32 devices in a mesh: dp: 8 (over z, y), shard: 4 (over x, core).
Axes of the slice: x: 2, y: 2, z: 4, core: 2. Of those that a mesh axis runs over, the one named last changes fastest.
Arguments:
- tokens: bfloat16 [2, 8, 1024, 576], P(None, 'dp', 'shard'), may hold values from -6 to 6
- segments: int32 [2, 8, 1024], P(None, 'dp', 'shard'), may hold values from 0 to 5, as said below
- attn_gain: bfloat16 [576], P('dp'), may hold values from 0.099609375 to 1.8984375
- query_weight: bfloat16 [576, 576], P('dp', 'shard'), may hold values from -0.25 to 0.25
- key_weight: bfloat16 [576, 192], P('dp', 'shard'), may hold values from -0.25 to 0.25
- value_weight: bfloat16 [576, 192], P('dp', 'shard'), may hold values from -0.25 to 0.25
- output_weight: bfloat16 [576, 576], P('shard', 'dp'), may hold values from -2 to 2
- mlp_gain: bfloat16 [576], P('dp'), may hold values from 0.099609375 to 1.8984375
- gate_weight: bfloat16 [576, 1536], P('dp', 'shard'), may hold values from -0.25 to 0.25
- up_weight: bfloat16 [576, 1536], P('dp', 'shard'), may hold values from -0.25 to 0.25
- down_weight: bfloat16 [1536, 576], P('shard', 'dp'), may hold values from -0.15625 to 0.15625
- out_grad: bfloat16 [2, 8, 1024, 576], P(None, 'dp', 'shard'), may hold values from -6 to 6
Outputs:
- out: bfloat16 [2, 8, 1024, 576], P(None, 'dp', 'shard')
- input_grad: bfloat16 [2, 8, 1024, 576], P(None, 'dp', 'shard')
- attn_gain_grad: float32 [576], P('dp')
- query_weight_grad: float32 [576, 576], P('dp', 'shard')
- key_weight_grad: float32 [576, 192], P('dp', 'shard')
- value_weight_grad: float32 [576, 192], P('dp', 'shard')
- output_weight_grad: float32 [576, 576], P('shard', 'dp')
- mlp_gain_grad: float32 [576], P('dp')
- gate_weight_grad: float32 [576, 1536], P('dp', 'shard')
- up_weight_grad: float32 [576, 1536], P('dp', 'shard')
- down_weight_grad: float32 [1536, 576], P('shard', 'dp')
The draws below stay inside these ranges and needn't reach their ends.
Inputs may be any that keep to these rules, and one draw needn't show every extreme that they name: `segments`: along each sequence the segment numbers start at 0 and never fall; every document but the last of its sequence has 204 tokens or more; for each index of dp one of its 2 sequences, drawn from the seed, is a single document; in every draw some sequence reaches the largest segment number.
All inputs are finite; a program needn't handle non-finite values.
Results may differ from the reference program's by a relative error of at most 0.02.
Values may be sent and summed in bfloat16 or wider, within the bound.
A program may use at most 128 MiB of HBM per device.

```python
import jax
import jax.numpy as jnp
from jax import lax

D = 576
H = 9
KV = 3
HD = 64
FF = 1536
LEN = 1024
MB = 2
NSEQ = 8
DOC_MIN = 204


def draw_segments(key, part):
    lengths_key, whole_key, column_key = jax.random.split(key, 3)
    pieces = LEN // DOC_MIN + 1
    doc_lengths = jax.random.randint(lengths_key, (MB, NSEQ, pieces), DOC_MIN, LEN + 1)
    doc_ends = jnp.cumsum(doc_lengths, axis=-1)
    token_index = jnp.arange(LEN)
    seg_ids = jnp.sum((doc_ends[:, :, None, :] <= token_index[None, None, :, None]).astype(jnp.int32), axis=-1)
    chosen = jax.random.randint(whole_key, (NSEQ,), 0, MB)
    single = jnp.arange(MB)[:, None] == chosen[None, :]
    packed_col = jax.random.randint(column_key, (), 0, NSEQ)
    packed_mb = (chosen[packed_col] + 1) % MB
    densest = (token_index // DOC_MIN).astype(jnp.int32)
    is_packed = (jnp.arange(MB)[:, None] == packed_mb) & (jnp.arange(NSEQ)[None, :] == packed_col)
    seg_ids = jnp.where(is_packed[:, :, None], densest[None, None, :], seg_ids)
    return jnp.where(single[:, :, None], 0, seg_ids).astype(jnp.int32)


def raised(values, key, source, target, parts, factor):
    owner, partner = [(jnp.arange(values.shape[dim]) // (values.shape[dim] // parts)).reshape([-1 if axis == dim else 1 for axis in range(values.ndim)]) for dim in (source, target)]
    chosen = jax.random.permutation(key, parts)[partner]
    strong = (owner == chosen) | (owner == (partner + parts // 2) % parts)
    return jnp.where(strong, factor * values, values)


def block_scale(key, dims, cuts, low, top_value):
    level = 1.0
    for axis_at, shards_of in cuts:
        heights = jax.random.uniform(jax.random.fold_in(jax.random.fold_in(key, 6), axis_at), (shards_of,), jnp.float32, low / len(cuts), top_value / len(cuts))
        level = level * jnp.repeat(jnp.exp(heights), dims[axis_at] // shards_of).reshape((-1,) + (1,) * (len(dims) - 1 - axis_at))
    return level


def noise(own_key, shape, width, bound, shards=(), held_as=jnp.bfloat16):
    factor_of = block_scale(own_key, shape, shards, -0.22, 0.18) if shards else 1.0
    array = jax.random.normal(own_key, shape, jnp.float32) * width * factor_of
    return jnp.minimum(jnp.maximum(array, -bound), bound).astype(held_as)


def noise_with(key, dims, spread, most, cuts, heavy, kind=jnp.bfloat16):
    result = spread * jax.random.normal(key, dims, jnp.float32)
    if cuts:
        result = result * block_scale(key, dims, cuts, -0.22, 0.18)
    return jnp.clip(raised(result, jax.random.fold_in(key, 3), *heavy), -most, most).astype(kind)


def setup_inputs(seed: int = 0) -> dict:
    key_of = jax.random.split(jax.random.key(seed), 13)
    tokens = noise_with(key_of[0], (MB, NSEQ, LEN, D), 1.0, 6.0, ((1, 8), (2, 4)), (1, 3, 8, 2.0))
    segments = draw_segments(jax.random.fold_in(key_of[12], 71), 0)
    attn_gain = jnp.clip(1.0 + 0.18 * jax.random.normal(key_of[2], (D,), jnp.float32), 0.099609375, 1.8984375).astype(jnp.bfloat16)
    query_weight = noise(key_of[3], (D, H * HD), D ** -0.5, 0.25, ((0, 8), (1, 4)))
    key_weight = noise(key_of[4], (D, KV * HD), D ** -0.5, 0.25, ((0, 8), (1, 4)))
    value_weight = noise(key_of[5], (D, KV * HD), D ** -0.5, 0.25, ((0, 8), (1, 4)))
    output_weight = noise(key_of[6], (H * HD, D), (max(D // 64, 1)) ** -0.5, 2.0, ((0, 4), (1, 8)))
    mlp_gain = jnp.clip(1.0 + 0.18 * jax.random.normal(key_of[7], (D,), jnp.float32), 0.099609375, 1.8984375).astype(jnp.bfloat16)
    gate_weight = noise(key_of[8], (D, FF), D ** -0.5, 0.25, ((0, 8), (1, 4)))
    up_weight = noise(key_of[9], (D, FF), D ** -0.5, 0.25, ((0, 8), (1, 4)))
    down_weight = noise(key_of[10], (FF, D), FF ** -0.5, 0.15625, ((0, 4), (1, 8)))
    out_grad = noise_with(key_of[11], (MB, NSEQ, LEN, D), 1.0, 6.0, ((1, 8), (2, 4)), (1, 3, 8, 2.0))
    return dict(tokens=tokens, segments=segments, attn_gain=attn_gain, query_weight=query_weight, key_weight=key_weight, value_weight=value_weight, output_weight=output_weight, mlp_gain=mlp_gain, gate_weight=gate_weight, up_weight=up_weight, down_weight=down_weight, out_grad=out_grad)


EPSILON = 1e-05
ROPE_BASE = 100000.0
MASKED = -1e+30

@jax.custom_vjp
def low(v):
    return lax.optimization_barrier(v.astype(jnp.bfloat16)).astype(jnp.float32)

@jax.custom_vjp
def low_back(v):
    return v

def low_keep(v):
    return (low(v), None)

def low_pass(kept, grad):
    return (grad,)

def back_keep(v):
    return (v, None)

def back_low(kept, grad):
    return (low(grad),)
low.defvjp(low_keep, low_pass)
low_back.defvjp(back_keep, back_low)

def highest(left_mat, right_mat):
    return jnp.dot(left_mat, right_mat, precision=lax.Precision.HIGHEST)

def rms_norm(inputs, gain_vec):
    inv_rms = lax.rsqrt(lax.optimization_barrier(jnp.mean(inputs * inputs, axis=-1, keepdims=True)) + EPSILON)
    return inputs * inv_rms * gain_vec

def rope_tables(positions):
    channel = jnp.arange(HD // 2).astype(jnp.float32)
    frequency = ROPE_BASE ** (-2.0 * channel / HD)
    angles = positions.astype(jnp.float32)[:, None] * frequency[None, :]
    return (jnp.cos(angles), jnp.sin(angles))

def rotate(vectors, cosine, sine_part):
    half_dim = HD // 2
    first_half = vectors[..., :half_dim]
    second_half = vectors[..., half_dim:]
    cos_wide = cosine[:, None, :]
    sin_wide = sine_part[:, None, :]
    return jnp.concatenate([first_half * cos_wide - second_half * sin_wide, second_half * cos_wide + first_half * sin_wide], axis=-1)

def sequence_layer(params, inputs, seg_ids):
    attn_gain, query_weight, key_weight, value_weight, output_weight, mlp_gain, gate_weight, up_weight, down_weight = params
    length = inputs.shape[0]
    token_index = jnp.arange(length, dtype=jnp.int32)
    earlier = lax.optimization_barrier(jnp.sum((seg_ids[None, :] < seg_ids[:, None]).astype(jnp.int32), axis=1))
    positions = token_index - earlier
    cosine, sine_part = rope_tables(positions)
    normed = low(rms_norm(inputs, attn_gain))
    queries = low_back(highest(normed, query_weight)).reshape(length, H, HD)
    queries = low(rotate(queries, cosine, sine_part)).reshape(length, KV, H // KV, HD)
    key_rot = low_back(highest(normed, key_weight)).reshape(length, KV, HD)
    key_rot = low(rotate(key_rot, cosine, sine_part))
    values = low(low_back(highest(normed, value_weight))).reshape(length, KV, HD)
    scores = jnp.einsum('tgrd,lgd->tgrl', queries, key_rot, precision=lax.Precision.HIGHEST) * HD ** (-0.5)
    allowed = (seg_ids[None, :] == seg_ids[:, None]) & (token_index[None, :] <= token_index[:, None])
    scores = jnp.where(allowed[:, None, None, :], low_back(scores), MASKED)
    soft_weights = low(jax.nn.softmax(scores, axis=-1))
    attended = jnp.einsum('tgrl,lgd->tgrd', soft_weights, values, precision=lax.Precision.HIGHEST).reshape(length, H * HD)
    attended = low(low_back(attended))
    mixed_sum = inputs + low_back(highest(attended, output_weight))
    normed_mlp = low(rms_norm(mixed_sum, mlp_gain))
    gate_act = low_back(highest(normed_mlp, gate_weight))
    upward = low_back(highest(normed_mlp, up_weight))
    hidden = low(jax.nn.silu(gate_act) * upward)
    return mixed_sum + low_back(highest(hidden, down_weight))

def reference(tokens, segments, attn_gain, query_weight, key_weight, value_weight, output_weight, mlp_gain, gate_weight, up_weight, down_weight, out_grad):
    seq_count = MB * NSEQ
    inputs = tokens.astype(jnp.float32).reshape(seq_count, LEN, D)
    seg_all = segments.reshape(seq_count, LEN)
    params = (attn_gain.astype(jnp.float32), query_weight.astype(jnp.float32), key_weight.astype(jnp.float32), value_weight.astype(jnp.float32), output_weight.astype(jnp.float32), mlp_gain.astype(jnp.float32), gate_weight.astype(jnp.float32), up_weight.astype(jnp.float32), down_weight.astype(jnp.float32))

    def forward(weight_set, layer_inputs):
        layer_fn = jax.checkpoint(sequence_layer)

        def scan_step(running, pair_in):
            return (running, layer_fn(weight_set, pair_in[0], pair_in[1]))
        running, outputs = lax.scan(scan_step, jnp.zeros((), jnp.float32), (layer_inputs, seg_all))
        return outputs
    outputs, pullback = jax.vjp(forward, params, inputs)
    param_grads, input_grads = pullback(out_grad.astype(jnp.float32).reshape(seq_count, LEN, D))
    full_shape = tokens.shape
    return (outputs.astype(jnp.bfloat16).reshape(full_shape), input_grads.astype(jnp.bfloat16).reshape(full_shape), param_grads[0], param_grads[1], param_grads[2], param_grads[3], param_grads[4], param_grads[5], param_grads[6], param_grads[7], param_grads[8])
```

```python
import jax
import jax.numpy as jnp
from jax import lax
from jax.experimental import pallas as pl
from jax.experimental.pallas import tpu as pltpu
from jax.sharding import PartitionSpec as P

D = 576
H = 9
KV = 3
HD = 64
FF = 1536


EPSILON = 1e-05
ROPE_BASE = 100000.0
MASKED = -1e30


def carried_in(value, axis, join, neutral):
    count, mine = (lax.axis_size(axis), lax.axis_index(axis))
    pieces = lax.all_gather(value, axis)
    total = jnp.full_like(value, 0) + jnp.asarray(neutral, value.dtype)

    def step(position, total):
        longer = join(total, pieces[position])
        return jnp.where(position < mine, longer, total)

    return lax.fori_loop(0, count - 1, step, total)


def collect(weights):
    query_w, key_w, value_w, output_w, gate_w, up_w, down_w, attn_g, mlp_g = weights
    rows_all = (
        lax.all_gather(query_w, "dp", axis=0, tiled=True),
        lax.all_gather(key_w, "dp", axis=0, tiled=True),
        lax.all_gather(value_w, "dp", axis=0, tiled=True),
        lax.all_gather(output_w, "dp", axis=1, tiled=True),
        lax.all_gather(gate_w, "dp", axis=0, tiled=True),
        lax.all_gather(up_w, "dp", axis=0, tiled=True),
        lax.all_gather(down_w, "dp", axis=1, tiled=True),
        lax.all_gather(attn_g, "dp", axis=0, tiled=True),
        lax.all_gather(mlp_g, "dp", axis=0, tiled=True),
    )
    whole_set = (
        lax.all_gather(rows_all[0], "shard", axis=1, tiled=True),
        lax.all_gather(rows_all[1], "shard", axis=1, tiled=True),
        lax.all_gather(rows_all[2], "shard", axis=1, tiled=True),
        lax.all_gather(rows_all[3], "shard", axis=0, tiled=True),
        lax.all_gather(rows_all[4], "shard", axis=1, tiled=True),
        lax.all_gather(rows_all[5], "shard", axis=1, tiled=True),
        lax.all_gather(rows_all[6], "shard", axis=0, tiled=True),
    )
    return (
        whole_set[0],
        whole_set[1],
        whole_set[2],
        whole_set[3],
        whole_set[4],
        whole_set[5],
        whole_set[6],
        rows_all[7].astype(jnp.float32),
        rows_all[8].astype(jnp.float32),
    )


def spread(grad_set):
    shard_count = lax.axis_size("shard")
    tiled_attn = jnp.broadcast_to(grad_set[7][:, None], (grad_set[7].shape[0], shard_count))
    tiled_mlp = jnp.broadcast_to(grad_set[8][:, None], (grad_set[8].shape[0], shard_count))
    cut_set = (
        lax.psum_scatter(
            grad_set[0].astype(jnp.bfloat16), "shard", scatter_dimension=1, tiled=True
        ).astype(jnp.float32),
        lax.psum_scatter(
            grad_set[1].astype(jnp.bfloat16), "shard", scatter_dimension=1, tiled=True
        ).astype(jnp.float32),
        lax.psum_scatter(
            grad_set[2].astype(jnp.bfloat16), "shard", scatter_dimension=1, tiled=True
        ).astype(jnp.float32),
        lax.psum_scatter(
            grad_set[3].astype(jnp.bfloat16), "shard", scatter_dimension=0, tiled=True
        ).astype(jnp.float32),
        lax.psum_scatter(
            grad_set[4].astype(jnp.bfloat16), "shard", scatter_dimension=1, tiled=True
        ).astype(jnp.float32),
        lax.psum_scatter(
            grad_set[5].astype(jnp.bfloat16), "shard", scatter_dimension=1, tiled=True
        ).astype(jnp.float32),
        lax.psum_scatter(
            grad_set[6].astype(jnp.bfloat16), "shard", scatter_dimension=0, tiled=True
        ).astype(jnp.float32),
        lax.psum_scatter(
            tiled_attn.astype(jnp.bfloat16), "shard", scatter_dimension=1, tiled=True
        ).astype(jnp.float32),
        lax.psum_scatter(
            tiled_mlp.astype(jnp.bfloat16), "shard", scatter_dimension=1, tiled=True
        ).astype(jnp.float32),
    )
    parts_set = (
        cut_set[0],
        cut_set[1],
        cut_set[2],
        cut_set[3],
        cut_set[4],
        cut_set[5],
        cut_set[6],
        cut_set[7][:, 0],
        cut_set[8][:, 0],
    )
    return (
        lax.psum_scatter(
            parts_set[0].astype(jnp.bfloat16), "dp", scatter_dimension=0, tiled=True
        ).astype(jnp.float32),
        lax.psum_scatter(
            parts_set[1].astype(jnp.bfloat16), "dp", scatter_dimension=0, tiled=True
        ).astype(jnp.float32),
        lax.psum_scatter(
            parts_set[2].astype(jnp.bfloat16), "dp", scatter_dimension=0, tiled=True
        ).astype(jnp.float32),
        lax.psum_scatter(
            parts_set[3].astype(jnp.bfloat16), "dp", scatter_dimension=1, tiled=True
        ).astype(jnp.float32),
        lax.psum_scatter(
            parts_set[4].astype(jnp.bfloat16), "dp", scatter_dimension=0, tiled=True
        ).astype(jnp.float32),
        lax.psum_scatter(
            parts_set[5].astype(jnp.bfloat16), "dp", scatter_dimension=0, tiled=True
        ).astype(jnp.float32),
        lax.psum_scatter(
            parts_set[6].astype(jnp.bfloat16), "dp", scatter_dimension=1, tiled=True
        ).astype(jnp.float32),
        lax.psum_scatter(
            parts_set[7].astype(jnp.bfloat16), "dp", scatter_dimension=0, tiled=True
        ).astype(jnp.float32),
        lax.psum_scatter(
            parts_set[8].astype(jnp.bfloat16), "dp", scatter_dimension=0, tiled=True
        ).astype(jnp.float32),
    )


RING = 8
LANES = 128
PIECE = 72
BLOCKS = 12
GAIN_ROWS = 16
ROWS = PIECE * BLOCKS + GAIN_ROWS
WIDTHS = (144, 48, 48, 144, 384, 384, 384)
GROUPS = (
    (0, 288, True, 4, 3),
    (288, 288, True, 3, 4),
    (576, 304, False, 4, 3),
)
MESH = pl.DeviceIdType.MESH


def ring_place():
    d = lax.axis_index("dp")
    s = lax.axis_index("shard")
    y, z = d % 2, d // 2
    p = z * (1 - y) + (7 - z) * y
    return p, d, s // 2, s % 2


def dp_of(p):
    p = (p + RING) % RING
    h = p // 4
    return 2 * p * (1 - h) + (15 - 2 * p) * h


def greet(places):
    barrier = pltpu.get_barrier_semaphore()
    for place in places:
        pl.semaphore_signal(barrier, inc=1, device_id=place, device_id_type=MESH)
    pl.semaphore_wait(barrier, len(places))


def gather_kernel(own, full, send_sem, ring_sem, x_sem, core_sem, own_sem):
    p, d, x, c = ring_place()
    right = (dp_of(p + 1), x * 2 + c)
    left = (dp_of(p - 1), x * 2 + c)
    across = (d, (1 - x) * 2 + c)
    sibling = (d, x * 2 + 1 - c)
    greet((right, left, across, sibling))
    sent = []

    def piece(group, origin, xs):
        first, rows = GROUPS[group][:2]
        return full.at[dp_of(origin), xs * 2 + c, pl.ds(first, rows), :]

    def push(source, target, sem, place):
        copy = pltpu.make_async_remote_copy(
            src_ref=source,
            dst_ref=target,
            send_sem=send_sem.at[len(sent)],
            recv_sem=sem,
            device_id=place,
            device_id_type=MESH,
        )
        copy.start()
        sent.append(copy)

    def arrived(target, sem):
        pltpu.make_async_remote_copy(
            src_ref=target,
            dst_ref=target,
            send_sem=send_sem.at[0],
            recv_sem=sem,
            device_id=sibling,
            device_id_type=MESH,
        ).wait_recv()

    def ring_push(group, at, origin, xs, lane, hop, rightward):
        slot = hop if rightward else 4 + hop
        place = right if rightward else left
        push(at, piece(group, origin, xs), ring_sem.at[group, slot, lane], place)

    own_copy = pltpu.make_async_copy(own, full.at[d, x * 2 + c], own_sem)
    own_copy.start()

    def own_piece(group):
        first, rows = GROUPS[group][:2]
        return own.at[pl.ds(first, rows), :]

    last_first = [g for g in range(len(GROUPS)) if not GROUPS[g][2]]
    ring_first = [g for g in range(len(GROUPS)) if GROUPS[g][2]]
    for g in last_first:
        push(own_piece(g), piece(g, p, x), x_sem.at[g, 0], across)
    for g in ring_first:
        ring_push(g, own_piece(g), p, x, 0, 1, True)
        ring_push(g, own_piece(g), p, x, 0, 1, False)
    for g in ring_first:
        push(own_piece(g), piece(g, p, x), x_sem.at[g, 0], across)
    for g in last_first:
        ring_push(g, own_piece(g), p, x, 0, 1, True)
        ring_push(g, own_piece(g), p, x, 0, 1, False)
    for g in range(len(GROUPS)):
        push(own_piece(g), piece(g, p, x), core_sem.at[g, 0, 0], sibling)
    for g in last_first:
        arrived(piece(g, p, 1 - x), x_sem.at[g, 0])
        ring_push(g, piece(g, p, 1 - x), p, 1 - x, 1, 1, True)
        ring_push(g, piece(g, p, 1 - x), p, 1 - x, 1, 1, False)
        push(piece(g, p, 1 - x), piece(g, p, 1 - x), core_sem.at[g, 0, 1], sibling)

    def slots(group, hop):
        if hop == 0:
            return [(0, p)]
        found = []
        if hop <= GROUPS[group][3]:
            found.append((hop, p - hop))
        if hop <= GROUPS[group][4]:
            found.append((4 + hop, p + hop))
        return found

    def from_across(hop):
        for g in ring_first:
            for slot, origin in slots(g, hop):
                here = piece(g, origin, 1 - x)
                arrived(here, x_sem.at[g, slot])
                push(here, here, core_sem.at[g, slot, 1], sibling)

    for hop in range(1, 5):
        for lane in range(2):
            for g in range(len(GROUPS)):
                if lane == 1 and g in ring_first:
                    continue
                xs = x if lane == 0 else 1 - x
                for slot, origin in slots(g, hop):
                    rightward = slot <= 4
                    here = piece(g, origin, xs)
                    arrived(here, ring_sem.at[g, slot, lane])
                    if hop < GROUPS[g][3 if rightward else 4]:
                        ring_push(g, here, origin, xs, lane, hop + 1, rightward)
                    if g in ring_first:
                        push(here, here, x_sem.at[g, slot], across)
                    push(here, here, core_sem.at[g, slot, lane], sibling)
        from_across(hop - 1)
    from_across(4)
    for g in range(len(GROUPS)):
        first, rows = GROUPS[g][:2]
        for hop in range(5):
            for slot, origin in slots(g, hop):
                for lane in range(2):
                    xs = x if lane == 0 else 1 - x
                    here = full.at[dp_of(origin), xs * 2 + 1 - c, pl.ds(first, rows), :]
                    arrived(here, core_sem.at[g, slot, lane])
    own_copy.wait()
    for copy in sent:
        copy.wait_send()


def ring_gather(own):
    groups = len(GROUPS)
    return pl.pallas_call(
        gather_kernel,
        out_shape=jax.ShapeDtypeStruct((RING, 4, ROWS, LANES), jnp.bfloat16),
        in_specs=[pl.BlockSpec(memory_space=pltpu.VMEM)],
        out_specs=pl.BlockSpec(memory_space=pltpu.VMEM),
        scratch_shapes=[
            pltpu.SemaphoreType.DMA((31 * groups,)),
            pltpu.SemaphoreType.DMA((groups, 9, 2)),
            pltpu.SemaphoreType.DMA((groups, 9)),
            pltpu.SemaphoreType.DMA((groups, 9, 2)),
            pltpu.SemaphoreType.DMA,
        ],
        compiler_params=pltpu.CompilerParams(
            collective_id=0, has_side_effects=True, vmem_limit_bytes=40 * 2**20
        ),
    )(own)


def scatter_kernel(
    terms, result, sums, from_core, from_x, from_ring, last, send_sem, ring_sem, x_sem, core_sem
):
    p, d, x, c = ring_place()
    right = (dp_of(p + 1), x * 2 + c)
    left = (dp_of(p - 1), x * 2 + c)
    across = (d, (1 - x) * 2 + c)
    sibling = (d, x * 2 + 1 - c)
    greet((right, left, across, sibling))
    sent = []

    def push(source, target, sem, place):
        copy = pltpu.make_async_remote_copy(
            src_ref=source,
            dst_ref=target,
            send_sem=send_sem.at[len(sent)],
            recv_sem=sem,
            device_id=place,
            device_id_type=MESH,
        )
        copy.start()
        sent.append(copy)

    def arrived(target, sem):
        pltpu.make_async_remote_copy(
            src_ref=target,
            dst_ref=target,
            send_sem=send_sem.at[0],
            recv_sem=sem,
            device_id=sibling,
            device_id_type=MESH,
        ).wait_recv()

    def slots(group, hop):
        if hop == 0:
            return [(0, p)]
        found = []
        if hop <= GROUPS[group][3]:
            found.append((hop, p + hop))
        if hop <= GROUPS[group][4]:
            found.append((4 + hop, p - hop))
        return found

    def wide(ref):
        return ref[...].astype(jnp.float32)

    def span(group):
        return pl.ds(GROUPS[group][0], GROUPS[group][1])

    order = (2, 0, 1)
    for hop in (4, 3, 2, 1, 0):
        for g in order:
            for slot, owner in slots(g, hop):
                for lane in range(2):
                    xs = 1 - x if lane == 0 else x
                    push(
                        terms.at[dp_of(owner), xs * 2 + 1 - c, span(g), :],
                        from_core.at[slot, lane, span(g), :],
                        core_sem.at[g, slot, lane],
                        sibling,
                    )

    def core_sum(g, slot, owner, lane):
        xs = 1 - x if lane == 0 else x
        landed = from_core.at[slot, lane, span(g), :]
        arrived(landed, core_sem.at[g, slot, lane])
        total = wide(terms.at[dp_of(owner), xs * 2 + c, span(g), :]) + wide(landed)
        sums[slot, lane, span(g), :] = total.astype(jnp.bfloat16)

    def ring_step(g, slot, hop, lane, buffer):
        rightward = slot <= 4
        most = GROUPS[g][3 if rightward else 4]
        held = buffer.at[slot, lane, span(g), :]
        if hop < most:
            landed = from_ring.at[slot, lane, span(g), :]
            arrived(landed, ring_sem.at[g, slot, lane])
            buffer[slot, lane, span(g), :] = (wide(held) + wide(landed)).astype(jnp.bfloat16)
        nearer = slot - 1 if hop > 1 else (0 if rightward else 9)
        push(
            held,
            from_ring.at[nearer, lane, span(g), :],
            ring_sem.at[g, nearer, lane],
            right if rightward else left,
        )

    def across_then_ring(g, hop):
        for slot, owner in slots(g, hop):
            landed = from_x.at[slot, span(g), :]
            arrived(landed, x_sem.at[g, slot])
            total = wide(sums.at[slot, 1, span(g), :]) + wide(landed)
            sums[slot, 1, span(g), :] = total.astype(jnp.bfloat16)
        if hop > 0:
            for slot, owner in slots(g, hop):
                ring_step(g, slot, hop, 1, sums)

    ring_first = [g for g in order if GROUPS[g][2]]
    for hop in (4, 3, 2, 1, 0):
        for g in order:
            for slot, owner in slots(g, hop):
                for lane in range(2):
                    core_sum(g, slot, owner, lane)
                    if g in ring_first:
                        if lane == 0:
                            push(
                                sums.at[slot, 0, span(g), :],
                                from_x.at[slot, span(g), :],
                                x_sem.at[g, slot],
                                across,
                            )
                    elif hop > 0:
                        ring_step(g, slot, hop, lane, sums)
        if hop < 4:
            for g in ring_first:
                across_then_ring(g, hop + 1)
    for g in order:
        if g in ring_first:
            continue
        for lane in range(2):
            total = wide(sums.at[0, lane, span(g), :])
            for slot in (0, 9):
                landed = from_ring.at[slot, lane, span(g), :]
                arrived(landed, ring_sem.at[g, slot, lane])
                total = total + wide(landed)
            if lane == 0:
                last[0, span(g), :] = total.astype(jnp.bfloat16)
                push(last.at[0, span(g), :], last.at[1, span(g), :], x_sem.at[g, 0], across)
            else:
                result[span(g), :] = total
    for g in ring_first:
        across_then_ring(g, 0)
        total = wide(sums.at[0, 1, span(g), :])
        for slot in (0, 9):
            landed = from_ring.at[slot, 1, span(g), :]
            arrived(landed, ring_sem.at[g, slot, 1])
            total = total + wide(landed)
        result[span(g), :] = total
    for g in order:
        if g in ring_first:
            continue
        arrived(last.at[1, span(g), :], x_sem.at[g, 0])
        result[span(g), :] = result[span(g), :] + wide(last.at[1, span(g), :])
    for copy in sent:
        copy.wait_send()


def ring_scatter(terms):
    groups = len(GROUPS)
    held = pltpu.VMEM((9, 2, ROWS, LANES), jnp.bfloat16)
    return pl.pallas_call(
        scatter_kernel,
        out_shape=jax.ShapeDtypeStruct((ROWS, LANES), jnp.float32),
        in_specs=[pl.BlockSpec(memory_space=pltpu.VMEM)],
        out_specs=pl.BlockSpec(memory_space=pltpu.VMEM),
        scratch_shapes=[
            held,
            held,
            pltpu.VMEM((9, ROWS, LANES), jnp.bfloat16),
            pltpu.VMEM((10, 2, ROWS, LANES), jnp.bfloat16),
            pltpu.VMEM((2, ROWS, LANES), jnp.bfloat16),
            pltpu.SemaphoreType.DMA((31 * groups,)),
            pltpu.SemaphoreType.DMA((groups, 10, 2)),
            pltpu.SemaphoreType.DMA((groups, 9)),
            pltpu.SemaphoreType.DMA((groups, 9, 2)),
        ],
        compiler_params=pltpu.CompilerParams(
            collective_id=1, has_side_effects=True, vmem_limit_bytes=48 * 2**20
        ),
    )(terms)


def ring_fits():
    return lax.axis_size("dp") == RING and lax.axis_size("shard") == 4


def collect_ring(weights):
    query_w, key_w, value_w, output_w, gate_w, up_w, down_w, attn_g, mlp_g = weights
    flat = jnp.concatenate([query_w, key_w, value_w, output_w.T, gate_w, up_w, down_w.T], axis=1)
    flat = flat.reshape(PIECE, BLOCKS, LANES).transpose(1, 0, 2).reshape(PIECE * BLOCKS, LANES)
    gains = jnp.pad(jnp.stack([attn_g, mlp_g]), ((0, GAIN_ROWS - 2), (0, LANES - PIECE)))
    full = ring_gather(jnp.concatenate([flat, gains], axis=0))
    wide = full[:, :, : PIECE * BLOCKS].reshape(RING, 4, BLOCKS, PIECE, LANES)
    wide = wide.transpose(0, 3, 1, 2, 4).reshape(D, 4, BLOCKS * LANES)
    found = []
    first = 0
    for width in WIDTHS:
        found.append(wide[:, :, first : first + width].reshape(D, 4 * width))
        first += width
    gain_set = full[:, 0, PIECE * BLOCKS :, :PIECE].astype(jnp.float32)
    return (
        found[0],
        found[1],
        found[2],
        found[3].T,
        found[4],
        found[5],
        found[6].T,
        gain_set[:, 0].reshape(D),
        gain_set[:, 1].reshape(D),
    )


def spread_ring(grad_set):
    terms = [grad_set[i].T if i in (3, 6) else grad_set[i] for i in range(7)]
    terms = [t.astype(jnp.bfloat16).reshape(D, 4, w) for t, w in zip(terms, WIDTHS)]
    flat = jnp.concatenate(terms, axis=2).reshape(RING, PIECE, 4, BLOCKS, LANES)
    flat = flat.transpose(0, 2, 3, 1, 4).reshape(RING, 4, PIECE * BLOCKS, LANES)
    gains = jnp.stack([grad_set[7], grad_set[8]]).astype(jnp.bfloat16).reshape(2, RING, PIECE)
    gains = jnp.pad(
        gains.transpose(1, 0, 2), ((0, 0), (0, GAIN_ROWS - 2), (0, LANES - PIECE))
    )
    gains = jnp.broadcast_to(gains[:, None], (RING, 4, GAIN_ROWS, LANES))
    cut = ring_scatter(jnp.concatenate([flat, gains], axis=2))
    wide = cut[: PIECE * BLOCKS].reshape(BLOCKS, PIECE, LANES).transpose(1, 0, 2)
    wide = wide.reshape(PIECE, BLOCKS * LANES)
    found = []
    first = 0
    for width in WIDTHS:
        found.append(wide[:, first : first + width])
        first += width
    return (
        found[0],
        found[1],
        found[2],
        found[3].T,
        found[4],
        found[5],
        found[6].T,
        cut[PIECE * BLOCKS, :PIECE],
        cut[PIECE * BLOCKS + 1, :PIECE],
    )


def rope_tables(positions):
    channel = jnp.arange(HD // 2).astype(jnp.float32)
    frequency = ROPE_BASE ** (-2.0 * channel / HD)
    angles = positions.astype(jnp.float32)[:, None] * frequency[None, :]
    return (jnp.cos(angles), jnp.sin(angles))


def rotate(vectors, cosine, sine_part):
    half_dim = HD // 2
    first_half = vectors[..., :half_dim]
    second_half = vectors[..., half_dim:]
    cos_wide = cosine[:, None, :]
    sin_wide = sine_part[:, None, :]
    return jnp.concatenate(
        [
            first_half * cos_wide - second_half * sin_wide,
            second_half * cos_wide + first_half * sin_wide,
        ],
        axis=-1,
    )


def unrotate(vectors, cosine, sine_part):
    half_dim = HD // 2
    first_half = vectors[..., :half_dim]
    second_half = vectors[..., half_dim:]
    cos_wide = cosine[:, None, :]
    sin_wide = sine_part[:, None, :]
    return jnp.concatenate(
        [
            first_half * cos_wide + second_half * sin_wide,
            second_half * cos_wide - first_half * sin_wide,
        ],
        axis=-1,
    )


def norm_forward(inputs):
    inv_rms = lax.rsqrt(jnp.mean(inputs * inputs, axis=-1, keepdims=True) + EPSILON)
    return (inputs * inv_rms, inv_rms)


def norm_backward(grad_out, unit_vals, inv_rms, gain_vec):
    scaled_grad = grad_out * gain_vec
    gain_grad = jnp.sum(grad_out * unit_vals, axis=0)
    input_part = inv_rms * (
        scaled_grad - unit_vals * jnp.mean(scaled_grad * unit_vals, axis=-1, keepdims=True)
    )
    return (input_part, gain_grad)


def inner_rows(left_mat, right_mat):
    return lax.dot_general(
        left_mat, right_mat, (((0,), (0,)), ((), ())), preferred_element_type=jnp.float32
    )


def inner_cols(left_mat, right_mat):
    return lax.dot_general(
        left_mat, right_mat, (((1,), (1,)), ((), ())), preferred_element_type=jnp.float32
    )


def per_device(
    tokens,
    segments,
    attn_gain,
    query_weight,
    key_weight,
    value_weight,
    output_weight,
    mlp_gain,
    gate_weight,
    up_weight,
    down_weight,
    out_grad,
):
    batches = tokens.shape[0]
    row_count = tokens.shape[2]
    shard_count = lax.axis_size("shard")
    seq_length = row_count * shard_count
    offset = lax.axis_index("shard") * row_count
    group_heads = H // KV
    score_scale = HD ** (-0.5)
    mlp_cols = FF
    seg_ids = segments[:, 0, :]
    local_index = jnp.arange(row_count, dtype=jnp.int32)
    global_index = offset + local_index
    before = jnp.sum((seg_ids[:, None, :] < seg_ids[:, :, None]).astype(jnp.int32), axis=2)
    local_start = offset + before
    tail_key = seg_ids[:, -1] * seq_length + (seq_length - 1 - local_start[:, -1])
    prefix = carried_in(tail_key, "shard", jnp.maximum, jnp.full((batches,), -1, jnp.int32))
    carried = (prefix[:, None] >= 0) & (prefix[:, None] // seq_length == seg_ids) & (before == 0)
    starts = jnp.where(carried, seq_length - 1 - prefix[:, None] % seq_length, local_start)
    positions = global_index[None, :] - starts
    key_index = jnp.arange(seq_length, dtype=jnp.int32)
    weights = (
        query_weight,
        key_weight,
        value_weight,
        output_weight,
        gate_weight,
        up_weight,
        down_weight,
        attn_gain,
        mlp_gain,
    )
    totals = [
        jnp.zeros((D, H * HD), jnp.float32),
        jnp.zeros((D, KV * HD), jnp.float32),
        jnp.zeros((D, KV * HD), jnp.float32),
        jnp.zeros((H * HD, D), jnp.float32),
        jnp.zeros((D, mlp_cols), jnp.float32),
        jnp.zeros((D, mlp_cols), jnp.float32),
        jnp.zeros((mlp_cols, D), jnp.float32),
        jnp.zeros((D,), jnp.float32),
        jnp.zeros((D,), jnp.float32),
    ]
    results = []
    input_grads = []
    whole_weights = collect_ring(weights) if ring_fits() else collect(weights)
    for micro_step in range(batches):
        forward_set = whole_weights
        (
            query_full,
            key_full,
            value_full,
            output_full,
            gate_full,
            up_full,
            down_full,
            attn_scale,
            mlp_scale,
        ) = forward_set
        inputs = tokens[micro_step, 0].astype(jnp.float32)
        grad_out = out_grad[micro_step, 0]
        cosine, sine_part = rope_tables(positions[micro_step])
        unit_attn, inv_attn = norm_forward(inputs)
        normed = (unit_attn * attn_scale).astype(jnp.bfloat16)
        query_raw = jnp.dot(normed, query_full, preferred_element_type=jnp.float32).reshape(
            row_count, H, HD
        )
        queries = (
            rotate(query_raw, cosine, sine_part)
            .astype(jnp.bfloat16)
            .reshape(row_count, KV, group_heads, HD)
        )
        key_raw = jnp.dot(normed, key_full, preferred_element_type=jnp.float32).reshape(
            row_count, KV, HD
        )
        key_rot = (
            rotate(key_raw, cosine, sine_part).astype(jnp.bfloat16).reshape(row_count, KV * HD)
        )
        value_low = jnp.dot(normed, value_full, preferred_element_type=jnp.float32).astype(
            jnp.bfloat16
        )
        key_all, value_all = (
            lax.all_gather(key_rot, "shard", axis=0, tiled=True),
            lax.all_gather(value_low, "shard", axis=0, tiled=True),
        )
        key_all = key_all.reshape(seq_length, KV, HD)
        value_all = value_all.reshape(seq_length, KV, HD)
        allowed = (key_index[None, :] >= starts[micro_step][:, None]) & (
            key_index[None, :] <= global_index[:, None]
        )

        def scores_of():
            raw_scores = (
                jnp.einsum("tgrd,lgd->tgrl", queries, key_all, preferred_element_type=jnp.float32)
                * score_scale
            )
            return jnp.where(allowed[:, None, None, :], raw_scores, MASKED)

        scores = scores_of()
        row_max = jnp.max(scores, axis=-1, keepdims=True)
        exp_terms = jnp.exp(scores - row_max)
        row_total = jnp.sum(exp_terms, axis=-1, keepdims=True)
        soft_weights = exp_terms / row_total
        log_total = row_max + jnp.log(row_total)
        soft_low = soft_weights.astype(jnp.bfloat16)
        attended = jnp.einsum(
            "tgrl,lgd->tgrd", soft_low, value_all, preferred_element_type=jnp.float32
        )
        attended = attended.reshape(row_count, H * HD).astype(jnp.bfloat16)
        mixed_sum = inputs + jnp.dot(attended, output_full, preferred_element_type=jnp.float32)
        unit_mlp, inv_mlp = norm_forward(mixed_sum)
        normed_mlp = (unit_mlp * mlp_scale).astype(jnp.bfloat16)
        gate_act = jnp.dot(normed_mlp, gate_full, preferred_element_type=jnp.float32)
        upward = jnp.dot(normed_mlp, up_full, preferred_element_type=jnp.float32)
        gate_sig = jax.nn.sigmoid(gate_act)
        hidden = (gate_act * gate_sig * upward).astype(jnp.bfloat16)
        down_terms = jnp.dot(hidden, down_full, preferred_element_type=jnp.float32)
        results.append((mixed_sum + down_terms).astype(jnp.bfloat16))
        backward_set = whole_weights
        (
            query_full,
            key_full,
            value_full,
            output_full,
            gate_full,
            up_full,
            down_full,
            attn_scale,
            mlp_scale,
        ) = backward_set
        grad_hidden = inner_cols(grad_out, down_full)
        totals[6] = totals[6] + inner_rows(hidden, grad_out)
        grad_gate = (grad_hidden * upward * gate_sig * (1.0 + gate_act * (1.0 - gate_sig))).astype(
            jnp.bfloat16
        )
        grad_up = (grad_hidden * gate_act * gate_sig).astype(jnp.bfloat16)
        totals[4] = totals[4] + inner_rows(normed_mlp, grad_gate)
        totals[5] = totals[5] + inner_rows(normed_mlp, grad_up)
        grad_terms = inner_cols(grad_gate, gate_full) + inner_cols(grad_up, up_full)
        mixed_part, mlp_gain_part = norm_backward(grad_terms, unit_mlp, inv_mlp, mlp_scale)
        totals[8] = totals[8] + mlp_gain_part
        grad_mixed = grad_out.astype(jnp.float32) + mixed_part
        grad_branch = grad_mixed.astype(jnp.bfloat16)
        totals[3] = totals[3] + inner_rows(attended, grad_branch)
        grad_attended = (
            inner_cols(grad_branch, output_full)
            .astype(jnp.bfloat16)
            .reshape(row_count, KV, group_heads, HD)
        )
        scores = scores_of()
        soft_weights = jnp.exp(scores - log_total)
        soft_low = soft_weights.astype(jnp.bfloat16)
        grad_soft = jnp.einsum(
            "tgrd,lgd->tgrl", grad_attended, value_all, preferred_element_type=jnp.float32
        )
        row_delta = jnp.sum(soft_weights * grad_soft, axis=-1, keepdims=True)
        grad_scores = (soft_weights * (grad_soft - row_delta)).astype(jnp.bfloat16)
        grad_queries = (
            jnp.einsum("tgrl,lgd->tgrd", grad_scores, key_all, preferred_element_type=jnp.float32)
            * score_scale
        )
        key_terms = (
            jnp.einsum("tgrl,tgrd->lgd", grad_scores, queries, preferred_element_type=jnp.float32)
            * score_scale
        )
        value_terms = jnp.einsum(
            "tgrl,tgrd->lgd", soft_low, grad_attended, preferred_element_type=jnp.float32
        )
        grad_keys, grad_values = (
            lax.psum_scatter(
                key_terms.reshape(seq_length, KV * HD).astype(jnp.bfloat16),
                "shard",
                scatter_dimension=0,
                tiled=True,
            ).astype(jnp.float32),
            lax.psum_scatter(
                value_terms.reshape(seq_length, KV * HD).astype(jnp.bfloat16),
                "shard",
                scatter_dimension=0,
                tiled=True,
            ).astype(jnp.float32),
        )
        grad_query_raw = (
            unrotate(grad_queries.reshape(row_count, H, HD), cosine, sine_part)
            .reshape(row_count, H * HD)
            .astype(jnp.bfloat16)
        )
        grad_key_raw = (
            unrotate(grad_keys.reshape(row_count, KV, HD), cosine, sine_part)
            .reshape(row_count, KV * HD)
            .astype(jnp.bfloat16)
        )
        grad_value_low = grad_values.astype(jnp.bfloat16)
        totals[0] = totals[0] + inner_rows(normed, grad_query_raw)
        totals[1] = totals[1] + inner_rows(normed, grad_key_raw)
        totals[2] = totals[2] + inner_rows(normed, grad_value_low)
        grad_normed_attn = (
            inner_cols(grad_query_raw, query_full)
            + inner_cols(grad_key_raw, key_full)
            + inner_cols(grad_value_low, value_full)
        )
        input_part, attn_gain_part = norm_backward(
            grad_normed_attn, unit_attn, inv_attn, attn_scale
        )
        totals[7] = totals[7] + attn_gain_part
        input_grads.append((grad_mixed + input_part).astype(jnp.bfloat16))
    shards = (spread_ring if ring_fits() else spread)(
        (
            totals[0],
            totals[1],
            totals[2],
            totals[3],
            totals[4],
            totals[5],
            totals[6],
            totals[7],
            totals[8],
        )
    )
    out_all = jnp.stack(results)[:, None]
    grads_all = jnp.stack(input_grads)[:, None]
    return (
        out_all,
        grads_all,
        shards[7],
        shards[0],
        shards[1],
        shards[2],
        shards[3],
        shards[8],
        shards[4],
        shards[5],
        shards[6],
    )


def solution(mesh):
    placed = (
        P(None, "dp", "shard", None),
        P(None, "dp", "shard"),
        P("dp"),
        P("dp", "shard"),
        P("dp", "shard"),
        P("dp", "shard"),
        P("shard", "dp"),
        P("dp"),
        P("dp", "shard"),
        P("dp", "shard"),
        P("shard", "dp"),
        P(None, "dp", "shard", None),
    )
    return jax.shard_map(
        per_device,
        mesh=mesh,
        in_specs=placed,
        out_specs=(
            P(None, "dp", "shard", None),
            P(None, "dp", "shard", None),
            P("dp"),
            P("dp", "shard"),
            P("dp", "shard"),
            P("dp", "shard"),
            P("shard", "dp"),
            P("dp"),
            P("dp", "shard"),
            P("dp", "shard"),
            P("shard", "dp"),
        ),
        check_vma=False,
    )
```

```python
import jax
import jax.numpy as jnp
from jax import lax
from jax.experimental import pallas as pl
from jax.experimental.pallas import tpu as pltpu
from jax.sharding import PartitionSpec as P

D = 576
H = 9
KV = 3
HD = 64
FF = 1536


EPSILON = 1e-05
ROPE_BASE = 100000.0
MASKED = -1e30


def carried_in(value, axis, join, neutral):
    count, mine = (lax.axis_size(axis), lax.axis_index(axis))
    pieces = lax.all_gather(value, axis)
    total = jnp.full_like(value, 0) + jnp.asarray(neutral, value.dtype)

    def step(position, total):
        longer = join(total, pieces[position])
        return jnp.where(position < mine, longer, total)

    return lax.fori_loop(0, count - 1, step, total)


def collect(weights):
    query_w, key_w, value_w, output_w, gate_w, up_w, down_w, attn_g, mlp_g = weights
    rows_all = (
        lax.all_gather(query_w, "dp", axis=0, tiled=True),
        lax.all_gather(key_w, "dp", axis=0, tiled=True),
        lax.all_gather(value_w, "dp", axis=0, tiled=True),
        lax.all_gather(output_w, "dp", axis=1, tiled=True),
        lax.all_gather(gate_w, "dp", axis=0, tiled=True),
        lax.all_gather(up_w, "dp", axis=0, tiled=True),
        lax.all_gather(down_w, "dp", axis=1, tiled=True),
        lax.all_gather(attn_g, "dp", axis=0, tiled=True),
        lax.all_gather(mlp_g, "dp", axis=0, tiled=True),
    )
    whole_set = (
        lax.all_gather(rows_all[0], "shard", axis=1, tiled=True),
        lax.all_gather(rows_all[1], "shard", axis=1, tiled=True),
        lax.all_gather(rows_all[2], "shard", axis=1, tiled=True),
        lax.all_gather(rows_all[3], "shard", axis=0, tiled=True),
        lax.all_gather(rows_all[4], "shard", axis=1, tiled=True),
        lax.all_gather(rows_all[5], "shard", axis=1, tiled=True),
        lax.all_gather(rows_all[6], "shard", axis=0, tiled=True),
    )
    return (
        whole_set[0],
        whole_set[1],
        whole_set[2],
        whole_set[3],
        whole_set[4],
        whole_set[5],
        whole_set[6],
        rows_all[7].astype(jnp.float32),
        rows_all[8].astype(jnp.float32),
    )


def spread(grad_set):
    shard_count = lax.axis_size("shard")
    tiled_attn = jnp.broadcast_to(grad_set[7][:, None], (grad_set[7].shape[0], shard_count))
    tiled_mlp = jnp.broadcast_to(grad_set[8][:, None], (grad_set[8].shape[0], shard_count))
    cut_set = (
        lax.psum_scatter(
            grad_set[0].astype(jnp.bfloat16), "shard", scatter_dimension=1, tiled=True
        ).astype(jnp.float32),
        lax.psum_scatter(
            grad_set[1].astype(jnp.bfloat16), "shard", scatter_dimension=1, tiled=True
        ).astype(jnp.float32),
        lax.psum_scatter(
            grad_set[2].astype(jnp.bfloat16), "shard", scatter_dimension=1, tiled=True
        ).astype(jnp.float32),
        lax.psum_scatter(
            grad_set[3].astype(jnp.bfloat16), "shard", scatter_dimension=0, tiled=True
        ).astype(jnp.float32),
        lax.psum_scatter(
            grad_set[4].astype(jnp.bfloat16), "shard", scatter_dimension=1, tiled=True
        ).astype(jnp.float32),
        lax.psum_scatter(
            grad_set[5].astype(jnp.bfloat16), "shard", scatter_dimension=1, tiled=True
        ).astype(jnp.float32),
        lax.psum_scatter(
            grad_set[6].astype(jnp.bfloat16), "shard", scatter_dimension=0, tiled=True
        ).astype(jnp.float32),
        lax.psum_scatter(
            tiled_attn.astype(jnp.bfloat16), "shard", scatter_dimension=1, tiled=True
        ).astype(jnp.float32),
        lax.psum_scatter(
            tiled_mlp.astype(jnp.bfloat16), "shard", scatter_dimension=1, tiled=True
        ).astype(jnp.float32),
    )
    parts_set = (
        cut_set[0],
        cut_set[1],
        cut_set[2],
        cut_set[3],
        cut_set[4],
        cut_set[5],
        cut_set[6],
        cut_set[7][:, 0],
        cut_set[8][:, 0],
    )
    return (
        lax.psum_scatter(
            parts_set[0].astype(jnp.bfloat16), "dp", scatter_dimension=0, tiled=True
        ).astype(jnp.float32),
        lax.psum_scatter(
            parts_set[1].astype(jnp.bfloat16), "dp", scatter_dimension=0, tiled=True
        ).astype(jnp.float32),
        lax.psum_scatter(
            parts_set[2].astype(jnp.bfloat16), "dp", scatter_dimension=0, tiled=True
        ).astype(jnp.float32),
        lax.psum_scatter(
            parts_set[3].astype(jnp.bfloat16), "dp", scatter_dimension=1, tiled=True
        ).astype(jnp.float32),
        lax.psum_scatter(
            parts_set[4].astype(jnp.bfloat16), "dp", scatter_dimension=0, tiled=True
        ).astype(jnp.float32),
        lax.psum_scatter(
            parts_set[5].astype(jnp.bfloat16), "dp", scatter_dimension=0, tiled=True
        ).astype(jnp.float32),
        lax.psum_scatter(
            parts_set[6].astype(jnp.bfloat16), "dp", scatter_dimension=1, tiled=True
        ).astype(jnp.float32),
        lax.psum_scatter(
            parts_set[7].astype(jnp.bfloat16), "dp", scatter_dimension=0, tiled=True
        ).astype(jnp.float32),
        lax.psum_scatter(
            parts_set[8].astype(jnp.bfloat16), "dp", scatter_dimension=0, tiled=True
        ).astype(jnp.float32),
    )


RING = 8
LANES = 128
PIECE = 72
BLOCKS = 12
GAIN_ROWS = 16
ROWS = PIECE * BLOCKS + GAIN_ROWS
WIDTHS = (144, 48, 48, 144, 384, 384, 384)
GROUPS = (
    (0, 288, True, 4, 3),
    (288, 288, True, 3, 4),
    (576, 304, False, 4, 3),
)
MESH = pl.DeviceIdType.MESH


def ring_place():
    d = lax.axis_index("dp")
    s = lax.axis_index("shard")
    y, z = d % 2, d // 2
    p = z * (1 - y) + (7 - z) * y
    return p, d, s // 2, s % 2


def dp_of(p):
    p = (p + RING) % RING
    h = p // 4
    return 2 * p * (1 - h) + (15 - 2 * p) * h


def greet(places):
    barrier = pltpu.get_barrier_semaphore()
    for place in places:
        pl.semaphore_signal(barrier, inc=1, device_id=place, device_id_type=MESH)
    pl.semaphore_wait(barrier, len(places))


def gather_kernel(own, full, send_sem, ring_sem, x_sem, core_sem, own_sem):
    p, d, x, c = ring_place()
    right = (dp_of(p + 1), x * 2 + c)
    left = (dp_of(p - 1), x * 2 + c)
    across = (d, (1 - x) * 2 + c)
    sibling = (d, x * 2 + 1 - c)
    greet((right, left, across, sibling))
    sent = []

    def piece(group, origin, xs):
        first, rows = GROUPS[group][:2]
        return full.at[dp_of(origin), xs * 2 + c, pl.ds(first, rows), :]

    def push(source, target, sem, place):
        copy = pltpu.make_async_remote_copy(
            src_ref=source,
            dst_ref=target,
            send_sem=send_sem.at[len(sent)],
            recv_sem=sem,
            device_id=place,
            device_id_type=MESH,
        )
        copy.start()
        sent.append(copy)

    def arrived(target, sem):
        pltpu.make_async_remote_copy(
            src_ref=target,
            dst_ref=target,
            send_sem=send_sem.at[0],
            recv_sem=sem,
            device_id=sibling,
            device_id_type=MESH,
        ).wait_recv()

    def ring_push(group, at, origin, xs, lane, hop, rightward):
        slot = hop if rightward else 4 + hop
        place = right if rightward else left
        push(at, piece(group, origin, xs), ring_sem.at[group, slot, lane], place)

    own_copy = pltpu.make_async_copy(own, full.at[d, x * 2 + c], own_sem)
    own_copy.start()

    def own_piece(group):
        first, rows = GROUPS[group][:2]
        return own.at[pl.ds(first, rows), :]

    last_first = [g for g in range(len(GROUPS)) if not GROUPS[g][2]]
    ring_first = [g for g in range(len(GROUPS)) if GROUPS[g][2]]
    for g in last_first:
        push(own_piece(g), piece(g, p, x), x_sem.at[g, 0], across)
    for g in ring_first:
        ring_push(g, own_piece(g), p, x, 0, 1, True)
        ring_push(g, own_piece(g), p, x, 0, 1, False)
    for g in ring_first:
        push(own_piece(g), piece(g, p, x), x_sem.at[g, 0], across)
    for g in last_first:
        ring_push(g, own_piece(g), p, x, 0, 1, True)
        ring_push(g, own_piece(g), p, x, 0, 1, False)
    for g in range(len(GROUPS)):
        push(own_piece(g), piece(g, p, x), core_sem.at[g, 0, 0], sibling)
    for g in last_first:
        arrived(piece(g, p, 1 - x), x_sem.at[g, 0])
        ring_push(g, piece(g, p, 1 - x), p, 1 - x, 1, 1, True)
        ring_push(g, piece(g, p, 1 - x), p, 1 - x, 1, 1, False)
        push(piece(g, p, 1 - x), piece(g, p, 1 - x), core_sem.at[g, 0, 1], sibling)

    def slots(group, hop):
        if hop == 0:
            return [(0, p)]
        found = []
        if hop <= GROUPS[group][3]:
            found.append((hop, p - hop))
        if hop <= GROUPS[group][4]:
            found.append((4 + hop, p + hop))
        return found

    def from_across(hop):
        for g in ring_first:
            for slot, origin in slots(g, hop):
                here = piece(g, origin, 1 - x)
                arrived(here, x_sem.at[g, slot])
                push(here, here, core_sem.at[g, slot, 1], sibling)

    for hop in range(1, 5):
        for lane in range(2):
            for g in range(len(GROUPS)):
                if lane == 1 and g in ring_first:
                    continue
                xs = x if lane == 0 else 1 - x
                for slot, origin in slots(g, hop):
                    rightward = slot <= 4
                    here = piece(g, origin, xs)
                    arrived(here, ring_sem.at[g, slot, lane])
                    if hop < GROUPS[g][3 if rightward else 4]:
                        ring_push(g, here, origin, xs, lane, hop + 1, rightward)
                    if g in ring_first:
                        push(here, here, x_sem.at[g, slot], across)
                    push(here, here, core_sem.at[g, slot, lane], sibling)
        from_across(hop - 1)
    from_across(4)
    for g in range(len(GROUPS)):
        first, rows = GROUPS[g][:2]
        for hop in range(5):
            for slot, origin in slots(g, hop):
                for lane in range(2):
                    xs = x if lane == 0 else 1 - x
                    here = full.at[dp_of(origin), xs * 2 + 1 - c, pl.ds(first, rows), :]
                    arrived(here, core_sem.at[g, slot, lane])
    own_copy.wait()
    for copy in sent:
        copy.wait_send()


def ring_gather(own):
    groups = len(GROUPS)
    return pl.pallas_call(
        gather_kernel,
        out_shape=jax.ShapeDtypeStruct((RING, 4, ROWS, LANES), jnp.bfloat16),
        in_specs=[pl.BlockSpec(memory_space=pltpu.VMEM)],
        out_specs=pl.BlockSpec(memory_space=pltpu.VMEM),
        scratch_shapes=[
            pltpu.SemaphoreType.DMA((31 * groups,)),
            pltpu.SemaphoreType.DMA((groups, 9, 2)),
            pltpu.SemaphoreType.DMA((groups, 9)),
            pltpu.SemaphoreType.DMA((groups, 9, 2)),
            pltpu.SemaphoreType.DMA,
        ],
        compiler_params=pltpu.CompilerParams(
            collective_id=0, has_side_effects=True, vmem_limit_bytes=40 * 2**20
        ),
    )(own)


def scatter_kernel(
    terms, result, sums, from_core, from_x, from_ring, last, send_sem, ring_sem, x_sem, core_sem
):
    p, d, x, c = ring_place()
    right = (dp_of(p + 1), x * 2 + c)
    left = (dp_of(p - 1), x * 2 + c)
    across = (d, (1 - x) * 2 + c)
    sibling = (d, x * 2 + 1 - c)
    greet((right, left, across, sibling))
    sent = []

    def push(source, target, sem, place):
        copy = pltpu.make_async_remote_copy(
            src_ref=source,
            dst_ref=target,
            send_sem=send_sem.at[len(sent)],
            recv_sem=sem,
            device_id=place,
            device_id_type=MESH,
        )
        copy.start()
        sent.append(copy)

    def arrived(target, sem):
        pltpu.make_async_remote_copy(
            src_ref=target,
            dst_ref=target,
            send_sem=send_sem.at[0],
            recv_sem=sem,
            device_id=sibling,
            device_id_type=MESH,
        ).wait_recv()

    def slots(group, hop):
        if hop == 0:
            return [(0, p)]
        found = []
        if hop <= GROUPS[group][3]:
            found.append((hop, p + hop))
        if hop <= GROUPS[group][4]:
            found.append((4 + hop, p - hop))
        return found

    def wide(ref):
        return ref[...].astype(jnp.float32)

    def span(group):
        return pl.ds(GROUPS[group][0], GROUPS[group][1])

    order = (2, 0, 1)
    for hop in (4, 3, 2, 1, 0):
        for g in order:
            for slot, owner in slots(g, hop):
                for lane in range(2):
                    xs = 1 - x if lane == 0 else x
                    push(
                        terms.at[dp_of(owner), xs * 2 + 1 - c, span(g), :],
                        from_core.at[slot, lane, span(g), :],
                        core_sem.at[g, slot, lane],
                        sibling,
                    )

    def core_sum(g, slot, owner, lane):
        xs = 1 - x if lane == 0 else x
        landed = from_core.at[slot, lane, span(g), :]
        arrived(landed, core_sem.at[g, slot, lane])
        total = wide(terms.at[dp_of(owner), xs * 2 + c, span(g), :]) + wide(landed)
        sums[slot, lane, span(g), :] = total.astype(jnp.bfloat16)

    def ring_step(g, slot, hop, lane, buffer):
        rightward = slot <= 4
        most = GROUPS[g][3 if rightward else 4]
        held = buffer.at[slot, lane, span(g), :]
        if hop < most:
            landed = from_ring.at[slot, lane, span(g), :]
            arrived(landed, ring_sem.at[g, slot, lane])
            buffer[slot, lane, span(g), :] = (wide(held) + wide(landed)).astype(jnp.bfloat16)
        nearer = slot - 1 if hop > 1 else (0 if rightward else 9)
        push(
            held,
            from_ring.at[nearer, lane, span(g), :],
            ring_sem.at[g, nearer, lane],
            right if rightward else left,
        )

    def across_then_ring(g, hop):
        for slot, owner in slots(g, hop):
            landed = from_x.at[slot, span(g), :]
            arrived(landed, x_sem.at[g, slot])
            total = wide(sums.at[slot, 1, span(g), :]) + wide(landed)
            sums[slot, 1, span(g), :] = total.astype(jnp.bfloat16)
        if hop > 0:
            for slot, owner in slots(g, hop):
                ring_step(g, slot, hop, 1, sums)

    ring_first = [g for g in order if GROUPS[g][2]]
    for hop in (4, 3, 2, 1, 0):
        for g in order:
            for slot, owner in slots(g, hop):
                for lane in range(2):
                    core_sum(g, slot, owner, lane)
                    if g in ring_first:
                        if lane == 0:
                            push(
                                sums.at[slot, 0, span(g), :],
                                from_x.at[slot, span(g), :],
                                x_sem.at[g, slot],
                                across,
                            )
                    elif hop > 0:
                        ring_step(g, slot, hop, lane, sums)
        if hop < 4:
            for g in ring_first:
                across_then_ring(g, hop + 1)
    for g in order:
        if g in ring_first:
            continue
        for lane in range(2):
            total = wide(sums.at[0, lane, span(g), :])
            for slot in (0, 9):
                landed = from_ring.at[slot, lane, span(g), :]
                arrived(landed, ring_sem.at[g, slot, lane])
                total = total + wide(landed)
            if lane == 0:
                last[0, span(g), :] = total.astype(jnp.bfloat16)
                push(last.at[0, span(g), :], last.at[1, span(g), :], x_sem.at[g, 0], across)
            else:
                result[span(g), :] = total
    for g in ring_first:
        across_then_ring(g, 0)
        total = wide(sums.at[0, 1, span(g), :])
        for slot in (0, 9):
            landed = from_ring.at[slot, 1, span(g), :]
            arrived(landed, ring_sem.at[g, slot, 1])
            total = total + wide(landed)
        result[span(g), :] = total
    for g in order:
        if g in ring_first:
            continue
        arrived(last.at[1, span(g), :], x_sem.at[g, 0])
        result[span(g), :] = result[span(g), :] + wide(last.at[1, span(g), :])
    for copy in sent:
        copy.wait_send()


def ring_scatter(terms):
    groups = len(GROUPS)
    held = pltpu.VMEM((9, 2, ROWS, LANES), jnp.bfloat16)
    return pl.pallas_call(
        scatter_kernel,
        out_shape=jax.ShapeDtypeStruct((ROWS, LANES), jnp.float32),
        in_specs=[pl.BlockSpec(memory_space=pltpu.VMEM)],
        out_specs=pl.BlockSpec(memory_space=pltpu.VMEM),
        scratch_shapes=[
            held,
            held,
            pltpu.VMEM((9, ROWS, LANES), jnp.bfloat16),
            pltpu.VMEM((10, 2, ROWS, LANES), jnp.bfloat16),
            pltpu.VMEM((2, ROWS, LANES), jnp.bfloat16),
            pltpu.SemaphoreType.DMA((31 * groups,)),
            pltpu.SemaphoreType.DMA((groups, 10, 2)),
            pltpu.SemaphoreType.DMA((groups, 9)),
            pltpu.SemaphoreType.DMA((groups, 9, 2)),
        ],
        compiler_params=pltpu.CompilerParams(
            collective_id=1, has_side_effects=True, vmem_limit_bytes=48 * 2**20
        ),
    )(terms)


def unpack_kernel(full, *outs):
    columns = [[] for _ in WIDTHS]
    for part in range(4):
        two = [full[i, part].astype(jnp.float32) for i in range(2)]
        blocks = [
            jnp.concatenate([t[b * PIECE : (b + 1) * PIECE] for t in two], axis=0)
            for b in range(BLOCKS)
        ]
        wide = jnp.concatenate(blocks[:3], axis=1)
        first = 0
        for i in range(4):
            columns[i].append(wide[:, first : first + WIDTHS[i]])
            first += WIDTHS[i]
        for i in range(4, 7):
            columns[i].extend(blocks[3 * i - 9 : 3 * i - 6])
    for out, found in zip(outs, columns):
        out[...] = jnp.concatenate(found, axis=1).astype(jnp.bfloat16)


def unpack(full):
    return pl.pallas_call(
        unpack_kernel,
        grid=(RING // 2,),
        out_shape=[jax.ShapeDtypeStruct((D, 4 * w), jnp.bfloat16) for w in WIDTHS],
        in_specs=[pl.BlockSpec((2, 4, ROWS, LANES), lambda i: (i, 0, 0, 0))],
        out_specs=[pl.BlockSpec((2 * PIECE, 4 * w), lambda i: (i, 0)) for w in WIDTHS],
        compiler_params=pltpu.CompilerParams(vmem_limit_bytes=40 * 2**20),
    )(full)


def pack_kernel(*refs):
    grads, gains, out = refs[:7], refs[7], refs[8]
    for part in range(4):
        cuts = [g[:, part * w : (part + 1) * w] for g, w in zip(grads, WIDTHS)]
        wide = jnp.concatenate(cuts[:4], axis=1)
        blocks = []
        for piece in [wide] + cuts[4:]:
            blocks += [piece[:, i * LANES : (i + 1) * LANES] for i in range(3)]
        out[0, part] = jnp.concatenate(blocks + [gains[0]], axis=0).astype(jnp.bfloat16)


def pack(terms, gains):
    return pl.pallas_call(
        pack_kernel,
        grid=(RING,),
        out_shape=jax.ShapeDtypeStruct((RING, 4, ROWS, LANES), jnp.bfloat16),
        in_specs=[pl.BlockSpec((PIECE, 4 * w), lambda i: (i, 0)) for w in WIDTHS]
        + [pl.BlockSpec((1, GAIN_ROWS, LANES), lambda i: (i, 0, 0))],
        out_specs=pl.BlockSpec((1, 4, ROWS, LANES), lambda i: (i, 0, 0, 0)),
        compiler_params=pltpu.CompilerParams(vmem_limit_bytes=40 * 2**20),
    )(*terms, gains)


def product(left_mat, right_mat, left_dim, right_dim):
    return lax.dot_general(
        left_mat,
        right_mat,
        (((left_dim,), (right_dim,)), ((), ())),
        preferred_element_type=jnp.float32,
    )


def masked_scores(queries, keys, starts, index):
    raw_scores = product(queries, keys, 1, 1) * HD ** (-0.5)
    column = lax.broadcasted_iota(jnp.int32, raw_scores.shape, 1)
    return jnp.where((column >= starts) & (column <= index), raw_scores, MASKED)


def attend_kernel(queries, both, starts, index, attended, log_total):
    count = starts.shape[1]
    keys, values = both[0, 0][:, :HD], both[0, 0][:, HD:]
    for r in range(H // KV):
        span = pl.ds(r * count, count)
        scores = masked_scores(queries[0, 0, span, :], keys, starts[0], index[...])
        row_max = jnp.max(scores, axis=-1, keepdims=True)
        exp_terms = jnp.exp(scores - row_max)
        row_total = jnp.sum(exp_terms, axis=-1, keepdims=True)
        soft_low = (exp_terms * (1.0 / row_total)).astype(jnp.bfloat16)
        attended[0, 0, span, :] = product(soft_low, values, 1, 0).astype(jnp.bfloat16)
        log_total[0, 0, span, :] = row_max + jnp.log(row_total)


def attend_back_kernel(
    queries, both, starts, index, log_total, grad_attended, grad_queries, grad_both
):
    count = starts.shape[1]
    keys, values = both[0, 0][:, :HD], both[0, 0][:, HD:]
    key_terms = jnp.zeros(keys.shape, jnp.float32)
    value_terms = jnp.zeros(keys.shape, jnp.float32)
    for r in range(H // KV):
        span = pl.ds(r * count, count)
        query, grad = queries[0, 0, span, :], grad_attended[0, 0, span, :]
        scores = masked_scores(query, keys, starts[0], index[...])
        soft_weights = jnp.exp(scores - log_total[0, 0, span, :])
        grad_soft = product(grad, values, 1, 1)
        row_delta = jnp.sum(soft_weights * grad_soft, axis=-1, keepdims=True)
        grad_scores = (soft_weights * (grad_soft - row_delta)).astype(jnp.bfloat16)
        grad_queries[0, 0, span, :] = product(grad_scores, keys, 1, 0) * HD ** (-0.5)
        key_terms += product(grad_scores, query, 0, 0)
        value_terms += product(soft_weights.astype(jnp.bfloat16), grad, 0, 0)
    grad_both[0, 0] = jnp.concatenate(
        [key_terms * HD ** (-0.5), value_terms], axis=1
    ).astype(jnp.bfloat16)


def head_specs(queries, both):
    def per_head(shape):
        return pl.BlockSpec((1, 1) + shape, lambda b, g: (b, g, 0, 0))

    wide, long = queries.shape[2], both.shape[2]
    count = wide * KV // H
    return (
        per_head((wide, HD)),
        per_head((long, 2 * HD)),
        pl.BlockSpec((1, count, 1), lambda b, g: (b, 0, 0)),
        pl.BlockSpec((count, 1), lambda b, g: (0, 0)),
        per_head((wide, 1)),
    )


def attend(queries, both, starts, index):
    query_at, both_at, starts_at, index_at, row_at = head_specs(queries, both)
    return pl.pallas_call(
        attend_kernel,
        grid=queries.shape[:2],
        out_shape=[
            jax.ShapeDtypeStruct(queries.shape, jnp.bfloat16),
            jax.ShapeDtypeStruct(queries.shape[:3] + (1,), jnp.float32),
        ],
        in_specs=[query_at, both_at, starts_at, index_at],
        out_specs=[query_at, row_at],
        compiler_params=pltpu.CompilerParams(vmem_limit_bytes=40 * 2**20),
    )(queries, both, starts, index)


def attend_back(queries, both, starts, index, log_total, grad_attended):
    query_at, both_at, starts_at, index_at, row_at = head_specs(queries, both)
    return pl.pallas_call(
        attend_back_kernel,
        grid=queries.shape[:2],
        out_shape=[
            jax.ShapeDtypeStruct(queries.shape, jnp.float32),
            jax.ShapeDtypeStruct(both.shape, jnp.bfloat16),
        ],
        in_specs=[query_at, both_at, starts_at, index_at, row_at, query_at],
        out_specs=[query_at, both_at],
        compiler_params=pltpu.CompilerParams(vmem_limit_bytes=40 * 2**20),
    )(queries, both, starts, index, log_total, grad_attended)


def ring_fits():
    return lax.axis_size("dp") == RING and lax.axis_size("shard") == 4


def collect_ring(weights):
    query_w, key_w, value_w, output_w, gate_w, up_w, down_w, attn_g, mlp_g = weights
    flat = jnp.concatenate([query_w, key_w, value_w, output_w.T, gate_w, up_w, down_w.T], axis=1)
    flat = flat.reshape(PIECE, BLOCKS, LANES).transpose(1, 0, 2).reshape(PIECE * BLOCKS, LANES)
    gains = jnp.pad(jnp.stack([attn_g, mlp_g]), ((0, GAIN_ROWS - 2), (0, LANES - PIECE)))
    full = ring_gather(jnp.concatenate([flat, gains], axis=0))
    found = unpack(full)
    gain_set = full[:, 0, PIECE * BLOCKS :, :PIECE].astype(jnp.float32)
    return (
        found[0],
        found[1],
        found[2],
        found[3].T,
        found[4],
        found[5],
        found[6].T,
        gain_set[:, 0].reshape(D),
        gain_set[:, 1].reshape(D),
    )


def spread_ring(grad_set):
    terms = [grad_set[i].T if i in (3, 6) else grad_set[i] for i in range(7)]
    gains = jnp.stack([grad_set[7], grad_set[8]]).reshape(2, RING, PIECE)
    gains = jnp.pad(
        gains.transpose(1, 0, 2), ((0, 0), (0, GAIN_ROWS - 2), (0, LANES - PIECE))
    )
    cut = ring_scatter(pack(terms, gains))
    wide = cut[: PIECE * BLOCKS].reshape(BLOCKS, PIECE, LANES).transpose(1, 0, 2)
    wide = wide.reshape(PIECE, BLOCKS * LANES)
    found = []
    first = 0
    for width in WIDTHS:
        found.append(wide[:, first : first + width])
        first += width
    return (
        found[0],
        found[1],
        found[2],
        found[3].T,
        found[4],
        found[5],
        found[6].T,
        cut[PIECE * BLOCKS, :PIECE],
        cut[PIECE * BLOCKS + 1, :PIECE],
    )


def rope_tables(positions):
    channel = jnp.arange(HD // 2).astype(jnp.float32)
    frequency = ROPE_BASE ** (-2.0 * channel / HD)
    angles = positions.astype(jnp.float32)[:, None] * frequency[None, :]
    return (jnp.cos(angles), jnp.sin(angles))


def rotate(vectors, cosine, sine_part):
    half_dim = HD // 2
    first_half = vectors[..., :half_dim]
    second_half = vectors[..., half_dim:]
    return jnp.concatenate(
        [
            first_half * cosine - second_half * sine_part,
            second_half * cosine + first_half * sine_part,
        ],
        axis=-1,
    )


def unrotate(vectors, cosine, sine_part):
    half_dim = HD // 2
    first_half = vectors[..., :half_dim]
    second_half = vectors[..., half_dim:]
    return jnp.concatenate(
        [
            first_half * cosine + second_half * sine_part,
            second_half * cosine - first_half * sine_part,
        ],
        axis=-1,
    )


def norm_forward(inputs):
    inv_rms = lax.rsqrt(jnp.mean(inputs * inputs, axis=-1, keepdims=True) + EPSILON)
    return (inputs * inv_rms, inv_rms)


def norm_backward(grad_out, unit_vals, inv_rms, gain_vec):
    scaled_grad = grad_out * gain_vec
    gain_grad = jnp.sum(grad_out * unit_vals, axis=0)
    input_part = inv_rms * (
        scaled_grad - unit_vals * jnp.mean(scaled_grad * unit_vals, axis=-1, keepdims=True)
    )
    return (input_part, gain_grad)


def inner_rows(left_mat, right_mat):
    return lax.dot_general(
        left_mat, right_mat, (((0,), (0,)), ((), ())), preferred_element_type=jnp.float32
    )


def inner_cols(left_mat, right_mat):
    return lax.dot_general(
        left_mat, right_mat, (((1,), (1,)), ((), ())), preferred_element_type=jnp.float32
    )


def per_device(
    tokens,
    segments,
    attn_gain,
    query_weight,
    key_weight,
    value_weight,
    output_weight,
    mlp_gain,
    gate_weight,
    up_weight,
    down_weight,
    out_grad,
):
    batches = tokens.shape[0]
    row_count = tokens.shape[2]
    shard_count = lax.axis_size("shard")
    seq_length = row_count * shard_count
    offset = lax.axis_index("shard") * row_count
    group_heads = H // KV
    seg_ids = segments[:, 0, :]
    local_index = jnp.arange(row_count, dtype=jnp.int32)
    global_index = offset + local_index
    before = jnp.sum((seg_ids[:, None, :] < seg_ids[:, :, None]).astype(jnp.int32), axis=2)
    local_start = offset + before
    tail_key = seg_ids[:, -1] * seq_length + (seq_length - 1 - local_start[:, -1])
    prefix = carried_in(tail_key, "shard", jnp.maximum, jnp.full((batches,), -1, jnp.int32))
    carried = (prefix[:, None] >= 0) & (prefix[:, None] // seq_length == seg_ids) & (before == 0)
    starts = jnp.where(carried, seq_length - 1 - prefix[:, None] % seq_length, local_start)
    positions = global_index[None, :] - starts
    weights = (
        query_weight,
        key_weight,
        value_weight,
        output_weight,
        gate_weight,
        up_weight,
        down_weight,
        attn_gain,
        mlp_gain,
    )
    (
        query_full,
        key_full,
        value_full,
        output_full,
        gate_full,
        up_full,
        down_full,
        attn_scale,
        mlp_scale,
    ) = collect_ring(weights) if ring_fits() else collect(weights)
    rows = batches * row_count

    def by_head(flat):
        return flat.reshape(batches, row_count, -1, HD).transpose(0, 2, 1, 3)

    def by_row(heads):
        return heads.reshape(batches, -1, row_count, HD).transpose(0, 2, 1, 3).reshape(rows, -1)

    def grouped(heads):
        return heads.reshape(batches, KV, group_heads * row_count, HD)

    inputs = tokens[:, 0].reshape(rows, D).astype(jnp.float32)
    grad_out = out_grad[:, 0].reshape(rows, D)
    cosine, sine_part = rope_tables(positions.reshape(rows))
    cosine = cosine.reshape(batches, 1, row_count, HD // 2)
    sine_part = sine_part.reshape(batches, 1, row_count, HD // 2)
    unit_attn, inv_attn = norm_forward(inputs)
    normed = (unit_attn * attn_scale).astype(jnp.bfloat16)
    key_rot = rotate(
        by_head(jnp.dot(normed, key_full, preferred_element_type=jnp.float32)), cosine, sine_part
    ).astype(jnp.bfloat16)
    value_low = by_head(
        jnp.dot(normed, value_full, preferred_element_type=jnp.float32).astype(jnp.bfloat16)
    )
    both = lax.all_gather(
        jnp.concatenate([key_rot, value_low], axis=-1), "shard", axis=2, tiled=True
    )
    queries = grouped(
        rotate(
            by_head(jnp.dot(normed, query_full, preferred_element_type=jnp.float32)),
            cosine,
            sine_part,
        ).astype(jnp.bfloat16)
    )
    starts_col, index_col = starts[:, :, None], global_index[:, None]
    attended, log_total = attend(queries, both, starts_col, index_col)
    attended = by_row(attended)
    mixed_sum = inputs + jnp.dot(attended, output_full, preferred_element_type=jnp.float32)
    unit_mlp, inv_mlp = norm_forward(mixed_sum)
    normed_mlp = (unit_mlp * mlp_scale).astype(jnp.bfloat16)
    gate_act = jnp.dot(normed_mlp, gate_full, preferred_element_type=jnp.float32)
    upward = jnp.dot(normed_mlp, up_full, preferred_element_type=jnp.float32)
    gate_sig = jax.nn.sigmoid(gate_act)
    hidden = (gate_act * gate_sig * upward).astype(jnp.bfloat16)
    down_terms = jnp.dot(hidden, down_full, preferred_element_type=jnp.float32)
    result = (mixed_sum + down_terms).astype(jnp.bfloat16)
    grad_hidden = inner_cols(grad_out, down_full)
    grad_gate = (grad_hidden * upward * gate_sig * (1.0 + gate_act * (1.0 - gate_sig))).astype(
        jnp.bfloat16
    )
    grad_up = (grad_hidden * gate_act * gate_sig).astype(jnp.bfloat16)
    grad_terms = inner_cols(grad_gate, gate_full) + inner_cols(grad_up, up_full)
    mixed_part, mlp_gain_part = norm_backward(grad_terms, unit_mlp, inv_mlp, mlp_scale)
    grad_mixed = grad_out.astype(jnp.float32) + mixed_part
    grad_branch = grad_mixed.astype(jnp.bfloat16)
    grad_attended = grouped(by_head(inner_cols(grad_branch, output_full).astype(jnp.bfloat16)))
    grad_queries, grad_both = attend_back(
        queries, both, starts_col, index_col, log_total, grad_attended
    )
    grad_both = lax.psum_scatter(
        grad_both,
        "shard",
        scatter_dimension=2,
        tiled=True,
    ).astype(jnp.float32)
    grad_queries = grad_queries.reshape(batches, H, row_count, HD)
    grad_query_raw = by_row(unrotate(grad_queries, cosine, sine_part).astype(jnp.bfloat16))
    grad_key_raw = by_row(
        unrotate(grad_both[..., :HD], cosine, sine_part).astype(jnp.bfloat16)
    )
    grad_value_low = by_row(grad_both[..., HD:].astype(jnp.bfloat16))
    grad_normed_attn = (
        inner_cols(grad_query_raw, query_full)
        + inner_cols(grad_key_raw, key_full)
        + inner_cols(grad_value_low, value_full)
    )
    input_part, attn_gain_part = norm_backward(grad_normed_attn, unit_attn, inv_attn, attn_scale)
    input_grad = (grad_mixed + input_part).astype(jnp.bfloat16)
    shards = (spread_ring if ring_fits() else spread)(
        (
            inner_rows(normed, grad_query_raw),
            inner_rows(normed, grad_key_raw),
            inner_rows(normed, grad_value_low),
            inner_rows(attended, grad_branch),
            inner_rows(normed_mlp, grad_gate),
            inner_rows(normed_mlp, grad_up),
            inner_rows(hidden, grad_out),
            attn_gain_part,
            mlp_gain_part,
        )
    )
    out_all = result.reshape(batches, 1, row_count, D)
    grads_all = input_grad.reshape(batches, 1, row_count, D)
    return (
        out_all,
        grads_all,
        shards[7],
        shards[0],
        shards[1],
        shards[2],
        shards[3],
        shards[8],
        shards[4],
        shards[5],
        shards[6],
    )


def solution(mesh):
    placed = (
        P(None, "dp", "shard", None),
        P(None, "dp", "shard"),
        P("dp"),
        P("dp", "shard"),
        P("dp", "shard"),
        P("dp", "shard"),
        P("shard", "dp"),
        P("dp"),
        P("dp", "shard"),
        P("dp", "shard"),
        P("shard", "dp"),
        P(None, "dp", "shard", None),
    )
    return jax.shard_map(
        per_device,
        mesh=mesh,
        in_specs=placed,
        out_specs=(
            P(None, "dp", "shard", None),
            P(None, "dp", "shard", None),
            P("dp"),
            P("dp", "shard"),
            P("dp", "shard"),
            P("dp", "shard"),
            P("shard", "dp"),
            P("dp"),
            P("dp", "shard"),
            P("dp", "shard"),
            P("shard", "dp"),
        ),
        check_vma=False,
    )
```
